32 devices in a mesh: group: 4 (over y, x), dev: 8 (over z, core).
Axes of the slice: x: 2, y: 2, z: 4, core: 2. Of those that a mesh axis runs over, the one named last changes fastest.
Arguments:
- embeddings: bfloat16 [40960, 768], P(('group', 'dev')), may hold values from -6 to 6
- projection: bfloat16 [256, 768], replicated, may hold values from -0.21875 to 0.21875
- triplets: int32 [3, 65536], P(None, ('group', 'dev')), may hold values from 0 to 1791, as said below
- cotangent: float32 [65536], P(('group', 'dev')), may hold values from -24 to 24
- wanted_rows: int32 [128, 128], P(('group', 'dev')), may hold values from -1 to 1279, as said below
Outputs:
- row_grad: bfloat16 [40960, 768], P(('group', 'dev'))
- weight_grad: float32 [256, 768], replicated
The draws below stay inside these ranges and needn't reach their ends.
Inputs may be any that keep to these rules, and one draw needn't show every extreme that they name: `wanted_rows`: in each list the live entries come first and are distinct rows of the owning device, the rest are -1; each list holds from 128 // 4 (at least 1) to 128 live entries; all lists of some group of requesters are full, and all lists sent to some group are full. `triplets`: anchors are below 1280; a positive or negative below 1280 is one of the device's own rows, else 1280 + h * 128 + s names a live slot s of the device's list for group h.
All inputs are finite; a program needn't handle non-finite values.
Results may differ from the reference program's by a relative error of at most 0.0058.
Values may be sent and summed in bfloat16 or wider, within the bound.
A program may use at most 64 MiB of HBM per device.

```python
import math
import jax
import jax.numpy as jnp
from jax import lax

D = 768
K = 256
ROWS_DEV = 1280
TRIP = 2048
SLOTS = 128
GROUPS = 4
MEMBERS = 8
ROWS = 40960
TRIPLETS = 65536


def pair_counts(key):
    total_devices = GROUPS * MEMBERS
    subkeys = jax.random.split(jax.random.fold_in(key, 11), 3)
    lowest = max(1, SLOTS // 4)
    counts = jax.random.randint(subkeys[0], (total_devices, GROUPS), lowest, SLOTS + 1)
    full_group = jax.random.randint(subkeys[1], (), 0, GROUPS)
    full_owner = jax.random.randint(subkeys[2], (), 0, GROUPS)
    device_group = jnp.arange(total_devices) // MEMBERS
    counts = jnp.where(device_group[:, None] == full_group, SLOTS, counts)
    counts = jnp.where(jnp.arange(GROUPS)[None, :] == full_owner, SLOTS, counts)
    return counts.astype(jnp.int32)


def draw_wanted_rows(key, part):
    counts = pair_counts(key)
    total_devices = GROUPS * MEMBERS
    subkeys = jax.random.split(jax.random.fold_in(key, 12), total_devices * GROUPS)
    orders = jax.vmap(lambda one_key: jax.random.permutation(one_key, ROWS_DEV))(subkeys)
    first_order = orders[0]
    first_order = jnp.where(first_order == ROWS_DEV - 1, first_order[0], first_order)
    first_order = first_order.at[0].set(ROWS_DEV - 1)
    orders = orders.at[0].set(first_order)
    chosen = orders[:, :SLOTS].reshape(total_devices, GROUPS, SLOTS)
    places = jnp.arange(SLOTS)
    listed = jnp.where(places[None, None, :] < counts[:, :, None], chosen, -1)
    return listed.reshape(total_devices * GROUPS, SLOTS).astype(jnp.int32)


def pick_rows(subkeys, counts, total_devices):
    shape = (total_devices, TRIP)
    own_choice = jax.random.randint(subkeys[0], shape, 0, ROWS_DEV)
    peer = jax.random.randint(subkeys[1], shape, 0, GROUPS)
    live = jnp.take_along_axis(counts, peer, axis=1)
    offset = jax.random.randint(subkeys[2], shape, 0, 1 << 20) % live
    remote = ROWS_DEV + peer * SLOTS + offset
    usage = jax.random.randint(subkeys[3], shape, 0, 4)
    return jnp.where(usage == 0, own_choice, remote)


def draw_triplets(key, part):
    counts = pair_counts(key)
    total_devices = GROUPS * MEMBERS
    subkeys = jax.random.split(jax.random.fold_in(key, 13), 9)
    anchors = jax.random.randint(subkeys[0], (total_devices, TRIP), 0, ROWS_DEV)
    positives = pick_rows(subkeys[1:5], counts, total_devices)
    negatives = pick_rows(subkeys[5:9], counts, total_devices)
    highest = ROWS_DEV + (GROUPS - 1) * SLOTS + counts[:, GROUPS - 1] - 1
    positives = positives.at[:, 0].set(highest)
    negatives = negatives.at[:, 0].set(ROWS_DEV - 1)
    stacked = jnp.stack([anchors, positives, negatives], axis=0)
    return stacked.reshape(3, total_devices * TRIP).astype(jnp.int32)


def block_scale(key, extent, cuts, least, largest):
    def one(position, blocks):
        steps = jax.random.uniform(jax.random.fold_in(jax.random.fold_in(key, 6), position), (blocks,), jnp.float32, least / len(cuts), largest / len(cuts))
        return jnp.repeat(jnp.exp(steps), extent[position] // blocks).reshape((-1,) + (1,) * (len(extent) - position - 1))

    level = one(*cuts[0])
    for cut in cuts[1:]:
        level = level * one(*cut)
    return level


def scatter_about(rng, dims, width, reach, cuts=(), kind=jnp.bfloat16):
    values = width * jax.random.normal(rng, dims, jnp.float32)
    if cuts:
        values = values * block_scale(rng, dims, cuts, -0.22, 0.18)
    return jnp.clip(values, -reach, reach).astype(kind)


def setup_inputs(seed: int = 0) -> dict:
    streams_of = jax.random.split(jax.random.key(seed), 6)
    embeddings = scatter_about(streams_of[0], (ROWS, D), 1.0, 6.0, ((0, 32),))
    projection = scatter_about(streams_of[1], (K, D), D ** -0.5, 0.21875)
    triplets = draw_triplets(jax.random.fold_in(streams_of[5], 71), 0)
    cotangent = scatter_about(streams_of[3], (TRIPLETS,), 4.0, 24.0, ((0, 32),), jnp.float32)
    wanted_rows = draw_wanted_rows(jax.random.fold_in(streams_of[5], 71), 0)
    return {"embeddings": embeddings, "projection": projection, "triplets": triplets, "cotangent": cotangent, "wanted_rows": wanted_rows}


distance_scale = 0.0625
margin = 1.0
pull_share = 0.5

def triplet_gradients(lookup, triple, cotangent):
    anchor_rows = lookup[triple[0]].astype(jnp.float32)
    positive_rows = lookup[triple[1]].astype(jnp.float32)
    negative_rows = lookup[triple[2]].astype(jnp.float32)
    to_positive = anchor_rows - positive_rows
    to_negative = anchor_rows - negative_rows
    near = distance_scale * lax.optimization_barrier(jnp.sum(to_positive * to_positive, axis=1))
    far = distance_scale * lax.optimization_barrier(jnp.sum(to_negative * to_negative, axis=1))
    hinge_gate = jax.nn.sigmoid(margin + near - far)
    pull_factor = 2.0 * distance_scale * cotangent * (1.0 - pull_share + pull_share * hinge_gate)
    push_factor = 2.0 * distance_scale * cotangent * pull_share * hinge_gate
    pull_term = pull_factor[:, None] * to_positive
    push_term = push_factor[:, None] * to_negative
    gradient = jnp.zeros(lookup.shape, jnp.float32)
    gradient = gradient.at[triple[0]].add(pull_term - push_term)
    gradient = gradient.at[triple[1]].add(-pull_term)
    gradient = gradient.at[triple[2]].add(push_term)
    return gradient

def reference(embeddings, projection, triplets, cotangent, wanted_rows):
    contract = (((1,), (1,)), ((), ()))
    projected = lax.dot_general(embeddings, projection, contract, preferred_element_type=jnp.float32).astype(jnp.bfloat16)
    total_devices = GROUPS * MEMBERS
    group_index = jnp.arange(GROUPS, dtype=jnp.int32)

    def accumulate(device, summed):
        member = device % MEMBERS
        first_row = (device * ROWS_DEV).astype(jnp.int32)
        wanted = lax.dynamic_slice_in_dim(wanted_rows, (device * GROUPS).astype(jnp.int32), GROUPS, 0)
        owners = ((group_index * MEMBERS + member) * ROWS_DEV)[:, None] + jnp.maximum(wanted, 0)
        owners = owners.reshape(-1).astype(jnp.int32)
        own_rows = lax.dynamic_slice_in_dim(projected, first_row, ROWS_DEV, 0)
        lookup = jnp.concatenate([own_rows, projected[owners]], axis=0)
        triple = lax.dynamic_slice_in_dim(triplets, (device * TRIP).astype(jnp.int32), TRIP, 1)
        weights_here = lax.dynamic_slice_in_dim(cotangent, (device * TRIP).astype(jnp.int32), TRIP, 0)
        gradient = triplet_gradients(lookup, triple, weights_here)
        current = lax.dynamic_slice_in_dim(summed, first_row, ROWS_DEV, 0)
        summed = lax.dynamic_update_slice_in_dim(summed, current + gradient[:ROWS_DEV], first_row, 0)
        remote_grad = lax.optimization_barrier(gradient[ROWS_DEV:].astype(jnp.bfloat16))
        return summed.at[owners].add(remote_grad.astype(jnp.float32))
    row_total = lax.fori_loop(0, total_devices, accumulate, jnp.zeros((ROWS, K), jnp.float32))
    row_rounded = row_total.astype(jnp.bfloat16)
    row_grad = jnp.dot(row_rounded, projection, preferred_element_type=jnp.float32).astype(jnp.bfloat16)
    weight_total = lax.dot_general(row_rounded, embeddings, (((0,), (0,)), ((), ())), preferred_element_type=jnp.float32)
    weight_grad = weight_total * (1.0 / math.sqrt(TRIPLETS))
    return (row_grad, weight_grad)
```

```python
import functools
import math

import jax
import jax.numpy as jnp
from jax import lax
from jax.experimental import pallas as pl
from jax.experimental.pallas import tpu as pltpu
from jax.sharding import PartitionSpec as P

distance_scale = 0.0625
margin = 1.0
pull_share = 0.5

MESH = pl.DeviceIdType.MESH
TILE = 256
NT = (((1,), (1,)), ((), ()))
TN = (((0,), (0,)), ((), ()))


def matmul(left, right, numbers=(((1,), (0,)), ((), ()))):
    return lax.dot_general(left, right, numbers, preferred_element_type=jnp.float32)


def indicator(hit):
    return jnp.where(hit, 1.0, 0.0)


def kernel(
    groups, layers, factor,
    emb_hbm, proj_ref, trip_ref, cot_ref, want_ref,
    row_hbm, weight_ref,
    emb, table, wanted, picks, served, fetched, fetched_flat,
    diff_pos, diff_neg, to_pos, to_neg, term_pos, term_neg,
    grad_own, grad_sent, grad_back, back_flat, rounded, row_out,
    partial, sent1, got1, sum2, sent2, got2, got3, final,
    load_sem, store_sem, want_send, want_recv, row_send, row_recv, back_send, back_recv,
    send1, recv1, send2, recv2, send3, recv3, send4, recv4, send5, recv5,
):
    shard_rows = emb.shape[0]
    rank = proj_ref.shape[0]
    triples = cot_ref.shape[1]
    slots = want_ref.shape[2]
    own_blocks = shard_rows // TILE
    far_blocks = groups * slots // TILE
    trip_blocks = triples // TILE
    pieces = final.shape[2]

    g = lax.axis_index("group")
    d = lax.axis_index("dev")
    z = d // 2
    core = d % 2
    sibling = z * 2 + (1 - core)

    load = pltpu.make_async_copy(emb_hbm, emb, load_sem)
    load.start()

    def peer_of(k):
        return lax.rem(g + k, groups)

    def layer_of(k):
        return lax.rem(z + k, layers)

    barrier = pltpu.get_barrier_semaphore()
    for k in range(1, groups):
        pl.semaphore_signal(barrier, inc=1, device_id=(peer_of(k), d), device_id_type=MESH)
    for k in range(1, layers):
        pl.semaphore_signal(
            barrier, inc=1, device_id=(g, layer_of(k) * 2 + core), device_id_type=MESH
        )
    pl.semaphore_signal(barrier, inc=1, device_id=(g, sibling), device_id_type=MESH)
    pl.semaphore_wait(barrier, groups - 1 + layers - 1 + 1)

    def send(source, target, send_sem, recv_sem, device):
        copy = pltpu.make_async_remote_copy(
            src_ref=source, dst_ref=target, send_sem=send_sem, recv_sem=recv_sem,
            device_id=device, device_id_type=MESH,
        )
        copy.start()
        return copy

    pending = []

    want_copies = []
    for k in range(1, groups):
        want_copies.append(send(
            want_ref.at[peer_of(k)], wanted.at[g], want_send.at[k], want_recv.at[k],
            (peer_of(k), d)))
    wanted[g] = want_ref[g]
    pending += want_copies

    load.wait()

    @pl.loop(0, own_blocks)
    def _(b):
        span = pl.ds(pl.multiple_of(b * TILE, TILE), TILE)
        table[:, span] = matmul(proj_ref[...], emb[span, :], NT).astype(jnp.bfloat16)

    for copy in want_copies:
        copy.wait_recv()

    @pl.loop(0, groups)
    def _(h):
        asked = jnp.maximum(wanted[h], 0)
        place = lax.broadcasted_iota(jnp.int32, (shard_rows, slots), 0)
        picks[h] = indicator(place == asked).astype(jnp.bfloat16)
        served[h] = matmul(table[:, :shard_rows], picks[h]).astype(jnp.bfloat16)

    row_copies = []
    for k in range(1, groups):
        row_copies.append(send(
            served.at[peer_of(k)], fetched.at[g], row_send.at[k], row_recv.at[k],
            (peer_of(k), d)))
    fetched[g] = served[g]
    pending += row_copies

    @pl.loop(0, trip_blocks)
    def _(t):
        cols = pl.ds(pl.multiple_of(t * TILE, TILE), TILE)
        anchor = trip_ref[0:1, cols]
        positive = trip_ref[1:2, cols]
        negative = trip_ref[2:3, cols]
        place = lax.broadcasted_iota(jnp.int32, (TILE, TILE), 0)

        @pl.loop(0, own_blocks)
        def _(b):
            first = pl.multiple_of(b * TILE, TILE)
            at_anchor = indicator(place == anchor - first)
            diff_pos[pl.ds(first, TILE), cols] = (
                at_anchor - indicator(place == positive - first)).astype(jnp.bfloat16)
            diff_neg[pl.ds(first, TILE), cols] = (
                at_anchor - indicator(place == negative - first)).astype(jnp.bfloat16)

        @pl.loop(own_blocks, own_blocks + far_blocks)
        def _(b):
            first = pl.multiple_of(b * TILE, TILE)
            diff_pos[pl.ds(first, TILE), cols] = (
                -indicator(place == positive - first)).astype(jnp.bfloat16)
            diff_neg[pl.ds(first, TILE), cols] = (
                -indicator(place == negative - first)).astype(jnp.bfloat16)

        to_pos[:, cols] = matmul(table[...], diff_pos[:shard_rows, cols])
        to_neg[:, cols] = matmul(table[...], diff_neg[:shard_rows, cols])

    for copy in row_copies:
        copy.wait_recv()
    for h in range(groups):
        fetched_flat[:, h * slots:(h + 1) * slots] = fetched[h]

    @pl.loop(0, trip_blocks)
    def _(t):
        cols = pl.ds(pl.multiple_of(t * TILE, TILE), TILE)
        toward = to_pos[:, cols] + matmul(fetched_flat[...], diff_pos[shard_rows:, cols])
        away = to_neg[:, cols] + matmul(fetched_flat[...], diff_neg[shard_rows:, cols])
        near = distance_scale * jnp.sum(toward * toward, axis=0, keepdims=True)
        far = distance_scale * jnp.sum(away * away, axis=0, keepdims=True)
        gate = jax.nn.sigmoid(margin + near - far)
        weight = 2.0 * distance_scale * cot_ref[:, cols]
        pull = weight * (1.0 - pull_share + pull_share * gate)
        push = weight * pull_share * gate
        term_pos[:, cols] = (pull * toward).astype(jnp.bfloat16)
        term_neg[:, cols] = (-push * away).astype(jnp.bfloat16)

    def scattered(b):
        rows = pl.ds(pl.multiple_of(b * TILE, TILE), TILE)
        return matmul(term_pos[...], diff_pos[rows, :], NT) + matmul(
            term_neg[...], diff_neg[rows, :], NT)

    each = TILE // slots

    @pl.loop(0, far_blocks)
    def _(b):
        block = scattered(b + own_blocks).astype(jnp.bfloat16)
        for part in range(each):
            grad_sent[b * each + part] = block[:, part * slots:(part + 1) * slots]

    back_copies = []
    for k in range(1, groups):
        back_copies.append(send(
            grad_sent.at[peer_of(k)], grad_back.at[g], back_send.at[k], back_recv.at[k],
            (peer_of(k), d)))
    grad_back[g] = grad_sent[g]
    pending += back_copies

    @pl.loop(0, own_blocks)
    def _(b):
        grad_own[b] = scattered(b)

    for copy in back_copies:
        copy.wait_recv()
    for h in range(groups):
        back_flat[:, h * slots:(h + 1) * slots] = grad_back[h]

    half = rank // 2
    partial[...] = jnp.zeros_like(partial)

    @pl.loop(0, own_blocks)
    def _(b):
        rows = pl.ds(pl.multiple_of(b * TILE, TILE), TILE)
        total = grad_own[b]
        for h in range(groups):
            total = total + matmul(grad_back[h], picks[h, rows, :], NT)
        block = total.astype(jnp.bfloat16)
        rounded[b] = block
        for part in range(2):
            partial[part] += matmul(block[part * half:(part + 1) * half, :], emb[rows, :])

    width = partial.shape[2] // 2
    bands = half // 16

    def cut(value):
        return [
            value[:, side * width:(side + 1) * width].reshape(bands, 16, width)
            for side in range(2)
        ]

    for side, value in enumerate(cut(partial[1 - core].astype(jnp.bfloat16))):
        sent1[side * bands:(side + 1) * bands] = value
    copy1 = send(sent1, got1, send1, recv1, (g, sibling))
    pending.append(copy1)

    def row_block(b):
        row_out[b] = matmul(rounded[b], proj_ref[...], TN).astype(jnp.bfloat16)
        rows = pl.ds(b * TILE, TILE)
        store = pltpu.make_async_copy(row_out.at[b], row_hbm.at[rows, :], store_sem.at[b])
        store.start()
        return store

    stores = [row_block(0)]
    kept = cut(partial[core])
    copy1.wait_recv()
    for side in range(2):
        whole = kept[side] + got1[side * bands:(side + 1) * bands].astype(jnp.float32)
        for band in range(bands):
            index = side * bands + band
            sum2[index // pieces, index % pieces] = whole[band]
            sent2[index // pieces, index % pieces] = whole[band].astype(jnp.bfloat16)

    copies2 = []
    for k in range(1, groups):
        copies2.append(send(
            sent2.at[peer_of(k)], got2.at[k], send2.at[k], recv2.at[k], (peer_of(k), d)))
    pending += copies2
    stores += [row_block(b) for b in range(1, (own_blocks + 1) // 2)]
    share = sum2[g]
    for k in range(1, groups):
        copies2[k - 1].wait_recv()
        share = share + got2[k].astype(jnp.float32)

    got3[z] = share.astype(jnp.bfloat16)
    copies3 = []
    for k in range(1, layers):
        copies3.append(send(
            got3.at[z], got3.at[z], send3.at[k], recv3.at[k], (g, layer_of(k) * 2 + core)))
    pending += copies3
    stores += [row_block(b) for b in range((own_blocks + 1) // 2, own_blocks)]
    for copy in copies3:
        copy.wait_recv()
    share = got3[0].astype(jnp.float32)
    for other in range(1, layers):
        share = share + got3[other].astype(jnp.float32)

    final[core, g] = share.astype(jnp.bfloat16)
    copies4 = []
    for k in range(1, groups):
        copies4.append(send(
            final.at[core, g], final.at[core, g], send4.at[k], recv4.at[k], (peer_of(k), d)))
    pending += copies4
    copies5 = []
    for k in range(groups):
        if k:
            copies4[k - 1].wait_recv()
        owner = lax.rem(g + groups - k, groups)
        copies5.append(send(
            final.at[core, owner], final.at[core, owner], send5.at[k], recv5.at[k],
            (g, sibling)))
    pending += copies5
    for copy in copies5:
        copy.wait_recv()
    for part in range(2):
        for index in range(2 * bands):
            side, band = index // bands, index % bands
            first = part * half + band * 16
            weight_ref[first:first + 16, side * width:(side + 1) * width] = (
                final[part, index // pieces, index % pieces].astype(jnp.float32) * factor)

    for store in stores:
        store.wait()
    for copy in pending:
        copy.wait_send()


def local(embeddings, projection, triplets, cotangent, wanted_rows):
    shard_rows, width = embeddings.shape
    rank = projection.shape[0]
    triples = cotangent.shape[0]
    groups = lax.axis_size("group")
    members = lax.axis_size("dev")
    layers = members // 2
    slots = wanted_rows.shape[1]
    table_rows = shard_rows + groups * slots
    bands = rank // 32
    pieces = 2 * bands // groups
    factor = 1.0 / math.sqrt(triples * groups * members)
    bf16, f32 = jnp.bfloat16, jnp.float32
    dma = pltpu.SemaphoreType.DMA
    share = (pieces, 16, width // 2)
    vmem = pltpu.VMEM
    scratch = [
        vmem((shard_rows, width), bf16),
        vmem((rank, shard_rows), bf16),
        vmem((groups, 1, slots), jnp.int32),
        vmem((groups, shard_rows, slots), bf16),
        vmem((groups, rank, slots), bf16),
        vmem((groups, rank, slots), bf16),
        vmem((rank, groups * slots), bf16),
        vmem((table_rows, triples), bf16),
        vmem((table_rows, triples), bf16),
        vmem((rank, triples), f32),
        vmem((rank, triples), f32),
        vmem((rank, triples), bf16),
        vmem((rank, triples), bf16),
        vmem((shard_rows // TILE, rank, TILE), f32),
        vmem((groups, rank, slots), bf16),
        vmem((groups, rank, slots), bf16),
        vmem((rank, groups * slots), bf16),
        vmem((shard_rows // TILE, rank, TILE), bf16),
        vmem((shard_rows // TILE, TILE, width), bf16),
        vmem((2, rank // 2, width), f32),
        vmem((2 * bands, 16, width // 2), bf16),
        vmem((2 * bands, 16, width // 2), bf16),
        vmem((groups,) + share, f32),
        vmem((groups,) + share, bf16),
        vmem((groups,) + share, bf16),
        vmem((layers,) + share, bf16),
        vmem((2, groups) + share, bf16),
        dma, dma((shard_rows // TILE,)),
        dma((groups,)), dma((groups,)), dma((groups,)), dma((groups,)),
        dma((groups,)), dma((groups,)),
        dma, dma, dma((groups,)), dma((groups,)), dma((layers,)), dma((layers,)),
        dma((groups,)), dma((groups,)), dma((groups,)), dma((groups,)),
    ]
    in_vmem = pl.BlockSpec(memory_space=pltpu.VMEM)
    anywhere = pl.BlockSpec(memory_space=pl.ANY)
    return pl.pallas_call(
        functools.partial(kernel, groups, layers, factor),
        out_shape=(
            jax.ShapeDtypeStruct((shard_rows, width), bf16),
            jax.ShapeDtypeStruct((rank, width), f32),
        ),
        in_specs=[anywhere, in_vmem, in_vmem, in_vmem, in_vmem],
        out_specs=(anywhere, in_vmem),
        scratch_shapes=scratch,
        compiler_params=pltpu.CompilerParams(
            collective_id=0, has_side_effects=True, vmem_limit_bytes=60 * 1024 * 1024
        ),
        cost_estimate=pl.CostEstimate(
            flops=10 * table_rows * triples * rank,
            bytes_accessed=4 * shard_rows * width,
            transcendentals=triples,
        ),
    )(
        embeddings, projection, triplets, cotangent.reshape(1, triples),
        wanted_rows.reshape(groups, 1, slots),
    )


def solution(mesh):
    return jax.shard_map(
        local,
        mesh=mesh,
        in_specs=(
            P(("group", "dev"), None),
            P(),
            P(None, ("group", "dev")),
            P(("group", "dev")),
            P(("group", "dev"), None),
        ),
        out_specs=(P(("group", "dev"), None), P()),
        check_vma=False,
    )
```

```python
import functools
import math

import jax
import jax.numpy as jnp
from jax import lax
from jax.experimental import pallas as pl
from jax.experimental.pallas import tpu as pltpu
from jax.sharding import PartitionSpec as P

distance_scale = 0.0625
margin = 1.0
pull_share = 0.5

MESH = pl.DeviceIdType.MESH
TILE = 256
LANES = 128
NT = (((1,), (1,)), ((), ()))


def matmul(left, right, numbers=(((1,), (0,)), ((), ()))):
    return lax.dot_general(left, right, numbers, preferred_element_type=jnp.float32)


def hits(place, index, first):
    return place == (index - first).astype(jnp.float32).astype(jnp.bfloat16)


def kernel(
    groups, layers,
    emb_hbm, proj_hbm, trip_hbm, cot_hbm, want_hbm,
    rounded_hbm, weight_hbm,
    emb, proj, trip, cot, table, wanted, picks, served, fetched, fetched_flat,
    diff, apart, terms, grad_own, grad_sent, grad_back, rounded, turned,
    partial, sent1, got1, sum2, sent2, got2, got3, final, summed,
    load_sem, store_sem, want_send, want_recv, row_send, row_recv, back_send, back_recv,
    send1, recv1, send2, recv2, send3, recv3, send4, recv4, send5, recv5,
):
    shard_rows = emb.shape[0]
    rank = proj.shape[0]
    triples = cot.shape[1]
    slots = wanted.shape[2]
    far_rows = groups * slots
    own_blocks = shard_rows // TILE
    far_blocks = far_rows // TILE
    trip_blocks = triples // TILE
    pieces = final.shape[2]
    bf16, f32 = jnp.bfloat16, jnp.float32

    g = lax.axis_index("group")
    d = lax.axis_index("dev")
    z = d // 2
    core = d % 2
    sibling = z * 2 + (1 - core)

    loads = []
    blocks = [slice(b * TILE, (b + 1) * TILE) for b in range(own_blocks)]
    for number, (source, target) in enumerate([
        (trip_hbm, trip), (want_hbm.at[g], wanted.at[g]), (cot_hbm, cot), (proj_hbm, proj),
    ] + [(emb_hbm.at[rows], emb.at[rows]) for rows in blocks]):
        loads.append(pltpu.make_async_copy(source, target, load_sem.at[number]))
        loads[-1].start()

    def peer_of(k):
        return lax.rem(g + k, groups)

    def layer_of(k):
        return lax.rem(z + k, layers)

    barrier = pltpu.get_barrier_semaphore()
    for k in range(1, groups):
        pl.semaphore_signal(barrier, inc=1, device_id=(peer_of(k), d), device_id_type=MESH)
    for k in range(1, layers):
        pl.semaphore_signal(
            barrier, inc=1, device_id=(g, layer_of(k) * 2 + core), device_id_type=MESH
        )
    pl.semaphore_signal(barrier, inc=1, device_id=(g, sibling), device_id_type=MESH)
    pl.semaphore_wait(barrier, groups - 1 + layers - 1 + 1)

    def send(source, target, send_sem, recv_sem, device):
        copy = pltpu.make_async_remote_copy(
            src_ref=source, dst_ref=target, send_sem=send_sem, recv_sem=recv_sem,
            device_id=device, device_id_type=MESH,
        )
        copy.start()
        return copy

    pending = []

    want_copies = []
    for k in range(1, groups):
        want_copies.append(send(
            want_hbm.at[peer_of(k)], wanted.at[g], want_send.at[k], want_recv.at[k],
            (peer_of(k), d)))
    pending += want_copies

    one = jnp.ones((), bf16)
    zero = jnp.zeros((), bf16)
    for load in loads[:3]:
        load.wait()

    def tile_parts(t):
        cols = pl.ds(pl.multiple_of(t * TILE, TILE), TILE)
        pair = pl.ds(pl.multiple_of(t * 2 * TILE, 2 * TILE), 2 * TILE)
        others = jnp.concatenate([trip[1:2, cols], trip[2:3, cols]], axis=1)
        place = lax.broadcasted_iota(jnp.int32, (TILE, TILE), 0).astype(f32).astype(bf16)
        return cols, pair, others, place, jnp.concatenate([place, place], axis=1)

    @pl.loop(0, trip_blocks)
    def _(t):
        cols, pair, others, place, wide = tile_parts(t)
        for b in range(own_blocks, own_blocks + far_blocks):
            first = b * TILE
            diff[first:first + TILE, pair] = jnp.where(hits(wide, others, first), -one, zero)

    loads[3].wait()
    for rows, load in zip(blocks, loads[4:]):
        load.wait()
        table[:, rows] = matmul(proj[...], emb[rows, :], NT).astype(bf16)

    for copy in want_copies:
        copy.wait_recv()

    narrow = lax.broadcasted_iota(jnp.int32, (TILE, slots), 0).astype(f32).astype(bf16)
    for h in range(groups):
        asked = jnp.maximum(wanted[h], 0)
        for b in range(own_blocks):
            picks[b * TILE:(b + 1) * TILE, h * slots:(h + 1) * slots] = jnp.where(
                hits(narrow, asked, b * TILE), one, zero)
    for b in range(far_blocks):
        block = matmul(table[...], picks[:, b * TILE:(b + 1) * TILE]).astype(bf16)
        for part in range(TILE // slots):
            served[b * (TILE // slots) + part] = block[:, part * slots:(part + 1) * slots]

    row_copies = []
    for k in range(1, groups):
        row_copies.append(send(
            served.at[peer_of(k)], fetched.at[g], row_send.at[k], row_recv.at[k],
            (peer_of(k), d)))
    fetched[g] = served[g]
    pending += row_copies

    def own_tile(t):
        cols, pair, others, place, wide = tile_parts(t)
        anchor = trip[0:1, cols]
        total = None
        for b in range(own_blocks):
            first = b * TILE
            at_anchor = jnp.where(hits(place, anchor, first), one, zero)
            block = jnp.concatenate([at_anchor, at_anchor], axis=1) - jnp.where(
                hits(wide, others, first), one, zero)
            diff[first:first + TILE, pair] = block
            term = matmul(table[:, first:first + TILE], block)
            total = term if total is None else total + term
        apart[:, pair] = total

    @pl.loop(0, trip_blocks // 2)
    def _(t):
        own_tile(2 * t)
        own_tile(2 * t + 1)

    for copy in row_copies:
        copy.wait_recv()
    for h in range(groups):
        fetched_flat[:, h * slots:(h + 1) * slots] = fetched[h]

    for t in range(trip_blocks):
        cols = slice(t * TILE, (t + 1) * TILE)
        pair = slice(t * 2 * TILE, (t + 1) * 2 * TILE)
        both = apart[:, pair] + matmul(fetched_flat[...], diff[shard_rows:, pair])
        squares = distance_scale * jnp.sum(both * both, axis=0, keepdims=True)
        gate = jax.nn.sigmoid(margin + squares[:, :TILE] - squares[:, TILE:])
        weight = 2.0 * distance_scale * cot[:, cols]
        pull = weight * (1.0 - pull_share + pull_share * gate)
        push = weight * pull_share * gate
        scale = jnp.concatenate([pull, -push], axis=1)
        terms[pair, :] = jnp.transpose((scale * both).astype(bf16))

    per = min(far_rows, 4 * slots)

    @pl.loop(0, far_rows // per)
    def _(b):
        rows = pl.ds(pl.multiple_of(shard_rows + b * per, slots), per)
        block = matmul(diff[rows, :], terms[...]).astype(bf16)
        grad_sent[pl.ds(b * (per // slots), per // slots)] = block.reshape(
            per // slots, slots, rank)

    back_copies = []
    for k in range(1, groups):
        back_copies.append(send(
            grad_sent.at[peer_of(k)], grad_back.at[g], back_send.at[k], back_recv.at[k],
            (peer_of(k), d)))
    grad_back[g] = grad_sent[g]
    pending += back_copies

    some = shard_rows // 2

    @pl.loop(0, 2)
    def _(b):
        rows = pl.ds(pl.multiple_of(b * some, some), some)
        grad_own[rows, :] = matmul(diff[rows, :], terms[...])

    for copy in back_copies:
        copy.wait_recv()
    returned = grad_back[...].reshape(far_rows, rank)
    for b in range(own_blocks):
        rows = slice(b * TILE, (b + 1) * TILE)
        block = (grad_own[rows, :] + matmul(picks[rows, :], returned)).astype(bf16)
        rounded[rows, :] = block
        turned[:, rows] = jnp.transpose(block)
    stores = [pltpu.make_async_copy(rounded, rounded_hbm, store_sem.at[0])]
    stores[0].start()

    half = rank // 2
    bands = half // 16
    span = 2 * LANES
    parts = range(emb.shape[1] // span)

    def cut(value):
        return [
            value[:, side * LANES:(side + 1) * LANES].reshape(bands, 16, LANES)
            for side in range(2)
        ]

    copies1 = []
    for s in parts:
        product = matmul(turned[...], emb[:, s * span:(s + 1) * span])
        partial[s, 0] = product[:half]
        partial[s, 1] = product[half:]
        for side, value in enumerate(cut(partial[s, 1 - core].astype(bf16))):
            sent1[s, side * bands:(side + 1) * bands] = value
        copies1.append(send(sent1.at[s], got1.at[s], send1.at[s], recv1.at[s], (g, sibling)))
    pending += copies1

    copies2 = {}
    for s in parts:
        kept = cut(partial[s, core])
        copies1[s].wait_recv()
        for side in range(2):
            whole = kept[side] + got1[s, side * bands:(side + 1) * bands].astype(f32)
            for band in range(bands):
                index = side * bands + band
                sum2[s, index // pieces, index % pieces] = whole[band]
                sent2[s, index // pieces, index % pieces] = whole[band].astype(bf16)
        for k in range(1, groups):
            copies2[s, k] = send(
                sent2.at[s, peer_of(k)], got2.at[s, k], send2.at[s, k], recv2.at[s, k],
                (peer_of(k), d))
    pending += list(copies2.values())

    copies3 = {}
    for s in parts:
        share = sum2[s, g]
        for k in range(1, groups):
            copies2[s, k].wait_recv()
            share = share + got2[s, k].astype(f32)
        got3[s, z] = share.astype(bf16)
        for k in range(1, layers):
            copies3[s, k] = send(
                got3.at[s, z], got3.at[s, z], send3.at[s, k], recv3.at[s, k],
                (g, layer_of(k) * 2 + core))
    pending += list(copies3.values())

    copies4 = {}
    copies5 = {}

    def forward(s, k):
        owner = lax.rem(g + groups - k, groups)
        copies5[s, k] = send(
            final.at[s, core, owner], final.at[s, core, owner], send5.at[s, k], recv5.at[s, k],
            (g, sibling))

    for s in parts:
        for k in range(1, layers):
            copies3[s, k].wait_recv()
        share = got3[s, 0].astype(f32)
        for other in range(1, layers):
            share = share + got3[s, other].astype(f32)
        final[s, core, g] = share.astype(bf16)
        for k in range(1, groups):
            copies4[s, k] = send(
                final.at[s, core, g], final.at[s, core, g], send4.at[s, k], recv4.at[s, k],
                (peer_of(k), d))
        forward(s, 0)
    pending += list(copies4.values())
    for s in parts:
        for k in range(1, groups):
            copies4[s, k].wait_recv()
            forward(s, k)
    pending += list(copies5.values())
    for s in parts:
        for k in range(groups):
            copies5[s, k].wait_recv()
        for part in range(2):
            for index in range(2 * bands):
                side, band = index // bands, index % bands
                row = part * half + band * 16
                column = s * span + side * LANES
                summed[row:row + 16, column:column + LANES] = (
                    final[s, part, index // pieces, index % pieces])
        columns = slice(s * span, (s + 1) * span)
        stores.append(pltpu.make_async_copy(
            summed.at[:, columns], weight_hbm.at[:, columns], store_sem.at[1 + s]))
        stores[-1].start()

    for store in stores:
        store.wait()
    for copy in pending:
        copy.wait_send()


def finish_kernel(
    factor, rounded_hbm, proj_hbm, weight_hbm, row_hbm, out_hbm,
    rounded, proj, weight, row, out, proj_sem, in_sem, row_sem, weight_sem, out_sem,
):
    blocks = rounded.shape[0] // TILE

    def copy(source, target, sem):
        made = pltpu.make_async_copy(source, target, sem)
        made.start()
        return made

    proj_load = copy(proj_hbm, proj, proj_sem)
    loads = []
    for b in range(blocks):
        rows = slice(b * TILE, (b + 1) * TILE)
        loads.append(copy(rounded_hbm.at[rows], rounded.at[rows], in_sem.at[b]))
    weight_load = copy(weight_hbm, weight, weight_sem)
    proj_load.wait()
    stores = []
    for b in range(blocks):
        rows = slice(b * TILE, (b + 1) * TILE)
        loads[b].wait()
        row[rows] = matmul(rounded[rows], proj[...]).astype(jnp.bfloat16)
        for part in range(2):
            some = slice(b * TILE + part * LANES, b * TILE + (part + 1) * LANES)
            stores.append(copy(row.at[some], row_hbm.at[some], row_sem.at[2 * b + part]))
    weight_load.wait()
    out[...] = weight[...].astype(jnp.float32) * factor
    stores.append(copy(out, out_hbm, out_sem))
    for store in stores:
        store.wait()


def local(embeddings, projection, triplets, cotangent, wanted_rows):
    shard_rows, width = embeddings.shape
    rank = projection.shape[0]
    triples = cotangent.shape[0]
    groups = lax.axis_size("group")
    members = lax.axis_size("dev")
    layers = members // 2
    slots = wanted_rows.shape[1]
    far_rows = groups * slots
    table_rows = shard_rows + far_rows
    bands = rank // 32
    pieces = 2 * bands // groups
    factor = 1.0 / math.sqrt(triples * groups * members)
    bf16, f32 = jnp.bfloat16, jnp.float32
    dma = pltpu.SemaphoreType.DMA
    share = (pieces, 16, LANES)
    parts = width // (2 * LANES)
    vmem = pltpu.VMEM
    scratch = [
        vmem((shard_rows, width), bf16),
        vmem((rank, width), bf16),
        vmem((3, triples), jnp.int32),
        vmem((1, triples), f32),
        vmem((rank, shard_rows), bf16),
        vmem((groups, 1, slots), jnp.int32),
        vmem((shard_rows, far_rows), bf16),
        vmem((groups, rank, slots), bf16),
        vmem((groups, rank, slots), bf16),
        vmem((rank, far_rows), bf16),
        vmem((table_rows, 2 * triples), bf16),
        vmem((rank, 2 * triples), f32),
        vmem((2 * triples, rank), bf16),
        vmem((shard_rows, rank), f32),
        vmem((groups, slots, rank), bf16),
        vmem((groups, slots, rank), bf16),
        vmem((shard_rows, rank), bf16),
        vmem((rank, shard_rows), bf16),
        vmem((parts, 2, rank // 2, 2 * LANES), f32),
        vmem((parts, 2 * bands, 16, LANES), bf16),
        vmem((parts, 2 * bands, 16, LANES), bf16),
        vmem((parts, groups) + share, f32),
        vmem((parts, groups) + share, bf16),
        vmem((parts, groups) + share, bf16),
        vmem((parts, layers) + share, bf16),
        vmem((parts, 2, groups) + share, bf16),
        vmem((rank, width), bf16),
        dma((4 + shard_rows // TILE,)), dma((1 + parts,)),
        dma((groups,)), dma((groups,)), dma((groups,)), dma((groups,)),
        dma((groups,)), dma((groups,)),
        dma((parts,)), dma((parts,)),
        dma((parts, groups)), dma((parts, groups)), dma((parts, layers)), dma((parts, layers)),
        dma((parts, groups)), dma((parts, groups)), dma((parts, groups)), dma((parts, groups)),
    ]
    anywhere = pl.BlockSpec(memory_space=pl.ANY)
    rounded, weight = pl.pallas_call(
        functools.partial(kernel, groups, layers),
        out_shape=(
            jax.ShapeDtypeStruct((shard_rows, rank), bf16),
            jax.ShapeDtypeStruct((rank, width), bf16),
        ),
        in_specs=[anywhere] * 5,
        out_specs=(anywhere, anywhere),
        scratch_shapes=scratch,
        compiler_params=pltpu.CompilerParams(
            collective_id=0, has_side_effects=True, vmem_limit_bytes=60 * 1024 * 1024
        ),
        cost_estimate=pl.CostEstimate(
            flops=10 * table_rows * triples * rank,
            bytes_accessed=4 * shard_rows * width,
            transcendentals=triples,
        ),
    )(
        embeddings, projection, triplets, cotangent.reshape(1, triples),
        wanted_rows.reshape(groups, 1, slots),
    )
    blocks = shard_rows // TILE
    return pl.pallas_call(
        functools.partial(finish_kernel, factor),
        out_shape=(
            jax.ShapeDtypeStruct((shard_rows, width), bf16),
            jax.ShapeDtypeStruct((rank, width), f32),
        ),
        in_specs=[anywhere] * 3,
        out_specs=(anywhere, anywhere),
        scratch_shapes=[
            vmem((shard_rows, rank), bf16), vmem((rank, width), bf16),
            vmem((rank, width), bf16), vmem((shard_rows, width), bf16),
            vmem((rank, width), f32),
            dma, dma((blocks,)), dma((2 * blocks,)), dma, dma,
        ],
        compiler_params=pltpu.CompilerParams(vmem_limit_bytes=60 * 1024 * 1024),
        cost_estimate=pl.CostEstimate(
            flops=2 * shard_rows * width * rank,
            bytes_accessed=2 * (shard_rows * (width + rank) + 4 * rank * width),
            transcendentals=0,
        ),
    )(rounded, projection, weight)


def solution(mesh):
    return jax.shard_map(
        local,
        mesh=mesh,
        in_specs=(
            P(("group", "dev"), None),
            P(),
            P(None, ("group", "dev")),
            P(("group", "dev")),
            P(("group", "dev"), None),
        ),
        out_specs=(P(("group", "dev"), None), P()),
        check_vma=False,
    )
```

```python
import functools
import math

import jax
import jax.numpy as jnp
from jax import lax
from jax.experimental import pallas as pl
from jax.experimental.pallas import tpu as pltpu
from jax.sharding import PartitionSpec as P

distance_scale = 0.0625
margin = 1.0
pull_share = 0.5

MESH = pl.DeviceIdType.MESH
TILE = 256
LANES = 128
NT = (((1,), (1,)), ((), ()))


def matmul(left, right, numbers=(((1,), (0,)), ((), ()))):
    return lax.dot_general(left, right, numbers, preferred_element_type=jnp.float32)


def hits(place, index, first):
    return place == (index - first).astype(jnp.float32).astype(jnp.bfloat16)


def kernel(
    groups, layers,
    emb_hbm, proj_hbm, trip_hbm, cot_hbm, want_hbm,
    rounded_hbm, weight_hbm,
    emb, proj, trip, cot, table, wanted, picks, served, fetched, fetched_flat,
    diff, apart, terms, grad_own, grad_sent, grad_back, rounded, turned,
    partial, sent1, got1, sum2, sent2, got2, got3, final, summed,
    load_sem, store_sem, want_send, want_recv, row_send, row_recv, back_send, back_recv,
    send1, recv1, send2, recv2, send3, recv3, send4, recv4, send5, recv5,
):
    shard_rows = emb.shape[0]
    rank = proj.shape[0]
    triples = cot.shape[1]
    slots = wanted.shape[2]
    far_rows = groups * slots
    own_blocks = shard_rows // TILE
    far_blocks = far_rows // TILE
    trip_blocks = triples // TILE
    pieces = final.shape[2]
    bf16, f32 = jnp.bfloat16, jnp.float32

    g = lax.axis_index("group")
    d = lax.axis_index("dev")
    z = d // 2
    core = d % 2
    sibling = z * 2 + (1 - core)

    loads = []
    blocks = [slice(b * TILE, (b + 1) * TILE) for b in range(own_blocks)]
    for number, (source, target) in enumerate([
        (trip_hbm, trip), (want_hbm.at[g], wanted.at[g]), (cot_hbm, cot), (proj_hbm, proj),
    ] + [(emb_hbm.at[rows], emb.at[rows]) for rows in blocks]):
        loads.append(pltpu.make_async_copy(source, target, load_sem.at[number]))
        loads[-1].start()

    def peer_of(k):
        return lax.rem(g + k, groups)

    def layer_of(k):
        return lax.rem(z + k, layers)

    barrier = pltpu.get_barrier_semaphore()
    for k in range(1, groups):
        pl.semaphore_signal(barrier, inc=1, device_id=(peer_of(k), d), device_id_type=MESH)
    for k in range(1, layers):
        pl.semaphore_signal(
            barrier, inc=1, device_id=(g, layer_of(k) * 2 + core), device_id_type=MESH
        )
    pl.semaphore_signal(barrier, inc=1, device_id=(g, sibling), device_id_type=MESH)
    pl.semaphore_wait(barrier, groups - 1 + layers - 1 + 1)

    def send(source, target, send_sem, recv_sem, device):
        copy = pltpu.make_async_remote_copy(
            src_ref=source, dst_ref=target, send_sem=send_sem, recv_sem=recv_sem,
            device_id=device, device_id_type=MESH,
        )
        copy.start()
        return copy

    pending = []

    want_copies = []
    for k in range(1, groups):
        want_copies.append(send(
            want_hbm.at[peer_of(k)], wanted.at[g], want_send.at[k], want_recv.at[k],
            (peer_of(k), d)))
    pending += want_copies

    one = jnp.ones((), bf16)
    zero = jnp.zeros((), bf16)
    for load in loads[:3]:
        load.wait()

    def tile_parts(t):
        cols = pl.ds(pl.multiple_of(t * TILE, TILE), TILE)
        pair = pl.ds(pl.multiple_of(t * 2 * TILE, 2 * TILE), 2 * TILE)
        others = jnp.concatenate([trip[1:2, cols], trip[2:3, cols]], axis=1)
        place = lax.broadcasted_iota(jnp.int32, (TILE, TILE), 0).astype(f32).astype(bf16)
        return cols, pair, others, place, jnp.concatenate([place, place], axis=1)

    @pl.loop(0, trip_blocks)
    def _(t):
        cols, pair, others, place, wide = tile_parts(t)
        for b in range(own_blocks, own_blocks + far_blocks):
            first = b * TILE
            diff[first:first + TILE, pair] = jnp.where(hits(wide, others, first), -one, zero)

    loads[3].wait()
    for rows, load in zip(blocks, loads[4:]):
        load.wait()
        table[:, rows] = matmul(proj[...], emb[rows, :], NT).astype(bf16)

    for copy in want_copies:
        copy.wait_recv()

    narrow = lax.broadcasted_iota(jnp.int32, (TILE, slots), 0).astype(f32).astype(bf16)
    for h in range(groups):
        asked = jnp.maximum(wanted[h], 0)
        for b in range(own_blocks):
            picks[b * TILE:(b + 1) * TILE, h * slots:(h + 1) * slots] = jnp.where(
                hits(narrow, asked, b * TILE), one, zero)
    for b in range(far_blocks):
        block = matmul(table[...], picks[:, b * TILE:(b + 1) * TILE]).astype(bf16)
        for part in range(TILE // slots):
            served[b * (TILE // slots) + part] = block[:, part * slots:(part + 1) * slots]

    row_copies = []
    for k in range(1, groups):
        row_copies.append(send(
            served.at[peer_of(k)], fetched.at[g], row_send.at[k], row_recv.at[k],
            (peer_of(k), d)))
    fetched[g] = served[g]
    pending += row_copies

    def own_tile(t):
        cols, pair, others, place, wide = tile_parts(t)
        anchor = trip[0:1, cols]
        total = None
        for b in range(own_blocks):
            first = b * TILE
            at_anchor = jnp.where(hits(place, anchor, first), one, zero)
            block = jnp.concatenate([at_anchor, at_anchor], axis=1) - jnp.where(
                hits(wide, others, first), one, zero)
            diff[first:first + TILE, pair] = block
            term = matmul(table[:, first:first + TILE], block)
            total = term if total is None else total + term
        apart[:, pair] = total

    @pl.loop(0, trip_blocks // 2)
    def _(t):
        own_tile(2 * t)
        own_tile(2 * t + 1)

    for copy in row_copies:
        copy.wait_recv()
    for h in range(groups):
        fetched_flat[:, h * slots:(h + 1) * slots] = fetched[h]

    for t in range(trip_blocks):
        cols = slice(t * TILE, (t + 1) * TILE)
        pair = slice(t * 2 * TILE, (t + 1) * 2 * TILE)
        both = apart[:, pair] + matmul(fetched_flat[...], diff[shard_rows:, pair])
        squares = distance_scale * jnp.sum(both * both, axis=0, keepdims=True)
        gate = jax.nn.sigmoid(margin + squares[:, :TILE] - squares[:, TILE:])
        weight = 2.0 * distance_scale * cot[:, cols]
        pull = weight * (1.0 - pull_share + pull_share * gate)
        push = weight * pull_share * gate
        scale = jnp.concatenate([pull, -push], axis=1)
        terms[pair, :] = jnp.transpose((scale * both).astype(bf16))

    per = min(far_rows, 4 * slots)

    @pl.loop(0, far_rows // per)
    def _(b):
        rows = pl.ds(pl.multiple_of(shard_rows + b * per, slots), per)
        block = matmul(diff[rows, :], terms[...]).astype(bf16)
        grad_sent[pl.ds(b * (per // slots), per // slots)] = block.reshape(
            per // slots, slots, rank)

    back_copies = []
    for k in range(1, groups):
        back_copies.append(send(
            grad_sent.at[peer_of(k)], grad_back.at[g], back_send.at[k], back_recv.at[k],
            (peer_of(k), d)))
    grad_back[g] = grad_sent[g]
    pending += back_copies

    grad_own[...] = matmul(diff[:shard_rows, :], terms[...])

    for copy in back_copies:
        copy.wait_recv()
    returned = grad_back[...].reshape(far_rows, rank)
    for b in range(own_blocks):
        rows = slice(b * TILE, (b + 1) * TILE)
        block = (grad_own[rows, :] + matmul(picks[rows, :], returned)).astype(bf16)
        rounded[rows, :] = block
        turned[:, rows] = jnp.transpose(block)
    stores = [pltpu.make_async_copy(rounded, rounded_hbm, store_sem.at[0])]
    stores[0].start()

    half = rank // 2
    bands = half // 16
    span = 2 * LANES
    parts = range(emb.shape[1] // span)

    def cut(value):
        return [
            value[:, side * LANES:(side + 1) * LANES].reshape(bands, 16, LANES)
            for side in range(2)
        ]

    copies1 = []
    for s in parts:
        product = matmul(turned[...], emb[:, s * span:(s + 1) * span])
        partial[s, 0] = product[:half]
        partial[s, 1] = product[half:]
        for side, value in enumerate(cut(partial[s, 1 - core].astype(bf16))):
            sent1[s, side * bands:(side + 1) * bands] = value
        copies1.append(send(sent1.at[s], got1.at[s], send1.at[s], recv1.at[s], (g, sibling)))
    pending += copies1

    copies2 = {}
    for s in parts:
        kept = cut(partial[s, core])
        copies1[s].wait_recv()
        for side in range(2):
            whole = kept[side] + got1[s, side * bands:(side + 1) * bands].astype(f32)
            for band in range(bands):
                index = side * bands + band
                sum2[s, index // pieces, index % pieces] = whole[band]
                sent2[s, index // pieces, index % pieces] = whole[band].astype(bf16)
        for k in range(1, groups):
            copies2[s, k] = send(
                sent2.at[s, peer_of(k)], got2.at[s, k], send2.at[s, k], recv2.at[s, k],
                (peer_of(k), d))
    pending += list(copies2.values())

    copies3 = {}
    for s in parts:
        share = sum2[s, g]
        for k in range(1, groups):
            copies2[s, k].wait_recv()
            share = share + got2[s, k].astype(f32)
        got3[s, z] = share.astype(bf16)
        for k in range(1, layers):
            copies3[s, k] = send(
                got3.at[s, z], got3.at[s, z], send3.at[s, k], recv3.at[s, k],
                (g, layer_of(k) * 2 + core))
    pending += list(copies3.values())

    copies4 = {}
    copies5 = {}

    def forward(s, k):
        owner = lax.rem(g + groups - k, groups)
        copies5[s, k] = send(
            final.at[s, core, owner], final.at[s, core, owner], send5.at[s, k], recv5.at[s, k],
            (g, sibling))

    for s in parts:
        for k in range(1, layers):
            copies3[s, k].wait_recv()
        share = got3[s, 0].astype(f32)
        for other in range(1, layers):
            share = share + got3[s, other].astype(f32)
        final[s, core, g] = share.astype(bf16)
        for k in range(1, groups):
            copies4[s, k] = send(
                final.at[s, core, g], final.at[s, core, g], send4.at[s, k], recv4.at[s, k],
                (peer_of(k), d))
        forward(s, 0)
    pending += list(copies4.values())
    for s in parts:
        for k in range(1, groups):
            copies4[s, k].wait_recv()
            forward(s, k)
    pending += list(copies5.values())
    for s in parts:
        for k in range(groups):
            copies5[s, k].wait_recv()
        for part in range(2):
            for index in range(2 * bands):
                side, band = index // bands, index % bands
                row = part * half + band * 16
                column = s * span + side * LANES
                summed[row:row + 16, column:column + LANES] = (
                    final[s, part, index // pieces, index % pieces])
        columns = slice(s * span, (s + 1) * span)
        stores.append(pltpu.make_async_copy(
            summed.at[:, columns], weight_hbm.at[:, columns], store_sem.at[1 + s]))
        stores[-1].start()

    for store in stores:
        store.wait()
    for copy in pending:
        copy.wait_send()


def finish_kernel(
    factor, rounded_hbm, proj_hbm, weight_hbm, row_hbm, out_hbm,
    rounded, proj, weight, row, out, proj_sem, in_sem, row_sem, weight_sem, out_sem,
):
    blocks = rounded.shape[0] // TILE

    def copy(source, target, sem):
        made = pltpu.make_async_copy(source, target, sem)
        made.start()
        return made

    proj_load = copy(proj_hbm, proj, proj_sem)
    loads = []
    for b in range(blocks):
        rows = slice(b * TILE, (b + 1) * TILE)
        loads.append(copy(rounded_hbm.at[rows], rounded.at[rows], in_sem.at[b]))
    weight_load = copy(weight_hbm, weight, weight_sem)
    proj_load.wait()
    stores = []
    for b in range(blocks):
        rows = slice(b * TILE, (b + 1) * TILE)
        loads[b].wait()
        row[rows] = matmul(rounded[rows], proj[...]).astype(jnp.bfloat16)
        for part in range(2):
            some = slice(b * TILE + part * LANES, b * TILE + (part + 1) * LANES)
            stores.append(copy(row.at[some], row_hbm.at[some], row_sem.at[2 * b + part]))
    weight_load.wait()
    out[...] = weight[...].astype(jnp.float32) * factor
    stores.append(copy(out, out_hbm, out_sem))
    for store in stores:
        store.wait()


def local(embeddings, projection, triplets, cotangent, wanted_rows):
    shard_rows, width = embeddings.shape
    rank = projection.shape[0]
    triples = cotangent.shape[0]
    groups = lax.axis_size("group")
    members = lax.axis_size("dev")
    layers = members // 2
    slots = wanted_rows.shape[1]
    far_rows = groups * slots
    table_rows = shard_rows + far_rows
    bands = rank // 32
    pieces = 2 * bands // groups
    factor = 1.0 / math.sqrt(triples * groups * members)
    bf16, f32 = jnp.bfloat16, jnp.float32
    dma = pltpu.SemaphoreType.DMA
    share = (pieces, 16, LANES)
    parts = width // (2 * LANES)
    vmem = pltpu.VMEM
    scratch = [
        vmem((shard_rows, width), bf16),
        vmem((rank, width), bf16),
        vmem((3, triples), jnp.int32),
        vmem((1, triples), f32),
        vmem((rank, shard_rows), bf16),
        vmem((groups, 1, slots), jnp.int32),
        vmem((shard_rows, far_rows), bf16),
        vmem((groups, rank, slots), bf16),
        vmem((groups, rank, slots), bf16),
        vmem((rank, far_rows), bf16),
        vmem((table_rows, 2 * triples), bf16),
        vmem((rank, 2 * triples), f32),
        vmem((2 * triples, rank), bf16),
        vmem((shard_rows, rank), f32),
        vmem((groups, slots, rank), bf16),
        vmem((groups, slots, rank), bf16),
        vmem((shard_rows, rank), bf16),
        vmem((rank, shard_rows), bf16),
        vmem((parts, 2, rank // 2, 2 * LANES), f32),
        vmem((parts, 2 * bands, 16, LANES), bf16),
        vmem((parts, 2 * bands, 16, LANES), bf16),
        vmem((parts, groups) + share, f32),
        vmem((parts, groups) + share, bf16),
        vmem((parts, groups) + share, bf16),
        vmem((parts, layers) + share, bf16),
        vmem((parts, 2, groups) + share, bf16),
        vmem((rank, width), bf16),
        dma((4 + shard_rows // TILE,)), dma((1 + parts,)),
        dma((groups,)), dma((groups,)), dma((groups,)), dma((groups,)),
        dma((groups,)), dma((groups,)),
        dma((parts,)), dma((parts,)),
        dma((parts, groups)), dma((parts, groups)), dma((parts, layers)), dma((parts, layers)),
        dma((parts, groups)), dma((parts, groups)), dma((parts, groups)), dma((parts, groups)),
    ]
    anywhere = pl.BlockSpec(memory_space=pl.ANY)
    rounded, weight = pl.pallas_call(
        functools.partial(kernel, groups, layers),
        out_shape=(
            jax.ShapeDtypeStruct((shard_rows, rank), bf16),
            jax.ShapeDtypeStruct((rank, width), bf16),
        ),
        in_specs=[anywhere] * 5,
        out_specs=(anywhere, anywhere),
        scratch_shapes=scratch,
        compiler_params=pltpu.CompilerParams(
            collective_id=0, has_side_effects=True, vmem_limit_bytes=60 * 1024 * 1024
        ),
        cost_estimate=pl.CostEstimate(
            flops=10 * table_rows * triples * rank,
            bytes_accessed=4 * shard_rows * width,
            transcendentals=triples,
        ),
    )(
        embeddings, projection, triplets, cotangent.reshape(1, triples),
        wanted_rows.reshape(groups, 1, slots),
    )
    blocks = shard_rows // TILE
    return pl.pallas_call(
        functools.partial(finish_kernel, factor),
        out_shape=(
            jax.ShapeDtypeStruct((shard_rows, width), bf16),
            jax.ShapeDtypeStruct((rank, width), f32),
        ),
        in_specs=[anywhere] * 3,
        out_specs=(anywhere, anywhere),
        scratch_shapes=[
            vmem((shard_rows, rank), bf16), vmem((rank, width), bf16),
            vmem((rank, width), bf16), vmem((shard_rows, width), bf16),
            vmem((rank, width), f32),
            dma, dma((blocks,)), dma((2 * blocks,)), dma, dma,
        ],
        compiler_params=pltpu.CompilerParams(vmem_limit_bytes=60 * 1024 * 1024),
        cost_estimate=pl.CostEstimate(
            flops=2 * shard_rows * width * rank,
            bytes_accessed=2 * (shard_rows * (width + rank) + 4 * rank * width),
            transcendentals=0,
        ),
    )(rounded, projection, weight)


def solution(mesh):
    return jax.shard_map(
        local,
        mesh=mesh,
        in_specs=(
            P(("group", "dev"), None),
            P(),
            P(None, ("group", "dev")),
            P(("group", "dev")),
            P(("group", "dev"), None),
        ),
        out_specs=(P(("group", "dev"), None), P()),
        check_vma=False,
    )
```
